32 devices in a mesh: groups: 2 (over x), gx: 16 (over z, y, core).
Axes of the slice: x: 2, y: 2, z: 4, core: 2. Of those that a mesh axis runs over, the one named last changes fastest.
Arguments:
- hidden: bfloat16 [39936, 768], P('gx', 'groups'), parts along dimension 1, may hold values from -6 to 6
- residual: bfloat16 [16384, 768], P('gx', 'groups'), parts along dimension 1, may hold values from -120 to 120
- w_down: bfloat16 [16, 19968, 2048], P('gx'), may hold values from -0.03125 to 0.03125
- gain: bfloat16 [16384], P('gx'), may hold values from 0.099609375 to 1.8984375
- w_qkv: bfloat16 [16, 2048, 5120], P('gx'), may hold values from -0.046875 to 0.046875
Outputs:
- stream: bfloat16 [16384, 768], P('gx', 'groups'), parts along dimension 1
- qkv: bfloat16 [10240, 768], P('gx', 'groups'), parts along dimension 1
The draws below stay inside these ranges and needn't reach their ends.
There are 2 independent parts, one for each index of `groups`. The reference program is written for one: setup_inputs(seed, part) draws one part's arguments, and reference() takes and returns one part's arrays. A program takes and returns all parts, laid end to end along the dimension named above; an argument that names none is the same for every part. Nothing has to cross between parts.
All inputs are finite; a program needn't handle non-finite values.
Results may differ from the reference program's by a relative error of at most 0.0058.
Values may be sent and summed in bfloat16 or wider, within the bound.
A program may use at most 192 MiB of HBM per device.

```python
import jax
import jax.numpy as jnp
from jax import lax

D = 16384
FFN_WIN = 39936
TOKENS = 384
XS = 8
YS = 2
QKV = 10240
N_GX = 16


def draw_residual(key, part):
    first, second, third = jax.random.split(jax.random.fold_in(key, 7), 3)
    position = jnp.arange(D, dtype=jnp.float32)[:, None] / D
    feature_scale = jnp.exp(jax.random.uniform(first, (D, 1), jnp.float32, jnp.log(0.3), jnp.log(3.0)))
    base = jnp.clip(jax.random.normal(second, (D, TOKENS), jnp.float32), -6.0, 6.0)
    ramp = jnp.sqrt(0.5 + position)
    token_scale = jnp.exp(jax.random.uniform(third, (1, TOKENS), jnp.float32, jnp.log(0.4), jnp.log(4.0)))
    return (base * feature_scale * ramp * token_scale).astype(jnp.bfloat16)


def block_levels(stream_key, extent, cuts, least, high):
    loudness = 1.0
    for dim, parts in cuts:
        steps = jax.random.uniform(jax.random.fold_in(jax.random.fold_in(stream_key, 6), dim), (parts,), jnp.float32, least / len(cuts), high / len(cuts))
        loudness = loudness * jnp.repeat(jnp.exp(steps), extent[dim] // parts).reshape((-1,) + (1,) * (len(extent) - 1 - dim))
    return loudness


def gaussian(rng, shape, scale, most, cuts=(), kind=jnp.bfloat16):
    level = block_levels(rng, shape, cuts, -0.22, 0.18) if cuts else 1.0
    result = jax.random.normal(rng, shape, jnp.float32) * scale * level
    return jnp.minimum(jnp.maximum(result, -most), most).astype(kind)


def setup_inputs(seed: int = 0, part: int = 0) -> dict:
    keys = jax.random.split(jax.random.key(seed), 6)
    part_keys = jax.random.split(jax.random.fold_in(keys[5], part), 6)
    hidden = gaussian(part_keys[0], (FFN_WIN, TOKENS), 1.0, 6.0, ((0, 16),))
    residual = draw_residual(jax.random.fold_in(jax.random.fold_in(keys[5], part), 71), part)
    w_down = gaussian(keys[2], (N_GX, FFN_WIN // YS, D // XS), FFN_WIN ** -0.5, 0.03125, ((0, 16),))
    gain = jnp.clip(1.0 + 0.18 * jax.random.normal(keys[3], (D,), jnp.float32), 0.099609375, 1.8984375).astype(jnp.bfloat16)
    w_qkv = gaussian(keys[4], (N_GX, D // XS, QKV // YS), D ** -0.5, 0.046875, ((0, 16),))
    return dict(hidden=hidden, residual=residual, w_down=w_down, gain=gain, w_qkv=w_qkv)


def reference(hidden, residual, w_down, gain, w_qkv):
    down_full = w_down.reshape(XS, YS, XS, FFN_WIN // N_GX, D // XS)
    down_full = down_full.transpose(2, 1, 3, 0, 4).reshape(FFN_WIN, D)
    qkv_full = w_qkv.reshape(XS, YS, D // XS, XS, QKV // N_GX)
    qkv_full = qkv_full.transpose(0, 2, 3, 1, 4).reshape(D, QKV)
    down = jnp.dot(down_full.T, hidden, preferred_element_type=jnp.float32)
    stream = (residual.astype(jnp.float32) + down).astype(jnp.bfloat16)
    values = stream.astype(jnp.float32)
    sumsq = lax.optimization_barrier(jnp.sum(values * values, axis=0))
    inv_rms = lax.rsqrt(sumsq / D + 1e-05)
    normed = (values * gain.astype(jnp.float32)[:, None] * inv_rms[None, :]).astype(jnp.bfloat16)
    qkv = jnp.dot(qkv_full.T, normed, preferred_element_type=jnp.float32).astype(jnp.bfloat16)
    return (stream, qkv)
```

```python
import functools

import jax
import jax.numpy as jnp
from jax import lax
from jax.experimental import pallas as pl
from jax.experimental.pallas import tpu as pltpu
from jax.sharding import PartitionSpec as P

D = 16384
XS = 8
MESH = pl.DeviceIdType.MESH


def swapped(block, axis, stride):
    count = lax.axis_size(axis)
    route = []
    for low in range(count):
        high = low | 1 << stride
        if high != low and high < count:
            route += [(low, high), (high, low)]
    return lax.ppermute(block, axis, route)


def for_sending(value):
    return jax.tree.map(lambda a: a.astype(jnp.bfloat16) if a.dtype == jnp.float32 else a, value)


def bit_of(dev_index, position):
    return dev_index // 2**position % 2


def collect_bits(current, positions, dev_index, send_fn):
    for position in positions:
        received = send_fn(current, position)
        high_bit = bit_of(dev_index, position) == 1
        current = jax.tree.map(
            lambda own_part, their_part: jnp.where(
                high_bit,
                jnp.concatenate([their_part, own_part], 0),
                jnp.concatenate([own_part, their_part], 0),
            ),
            current,
            received,
        )
    return current


def halve_bits(partial_value, first_bit, bit_count, bit_order, dev_index, send_fn):
    trailing = partial_value.shape[1:]
    shaped = partial_value.reshape(
        (2,) * bit_count + (partial_value.shape[0] // 2**bit_count,) + trailing
    )
    remaining = list(range(bit_count - 1, -1, -1))
    for relative in bit_order:
        axis_pos = sum([1 for other in remaining if other > relative])
        high_bit = bit_of(dev_index, first_bit + relative)
        retained = lax.dynamic_index_in_dim(shaped, high_bit, axis_pos, keepdims=False)
        outgoing = lax.dynamic_index_in_dim(shaped, 1 - high_bit, axis_pos, keepdims=False)
        shaped = retained + send_fn(outgoing, first_bit + relative)
        remaining = [other for other in remaining if other != relative]
    return shaped


def permuted(hidden, residual, w_down, gain, w_qkv):
    dev_index = lax.axis_index("gx")
    y_bits = (lax.axis_size("gx") // XS).bit_length() - 1
    x_bits = XS.bit_length() - 1
    x_positions = list(range(y_bits, y_bits + x_bits))
    y_positions = list(range(y_bits))
    tile_down = w_down[0]
    tile_qkv = w_qkv[0]
    gathered = collect_bits(
        hidden, x_positions, dev_index, lambda current, position: swapped(current, "gx", position)
    )
    partial_down = lax.dot_general(
        tile_down, gathered, (((0,), (0,)), ((), ())), preferred_element_type=jnp.float32
    )
    down_order = list(range(y_bits - 1, -1, -1))
    down = halve_bits(
        partial_down,
        0,
        y_bits,
        down_order,
        dev_index,
        lambda current, position: swapped(current, "gx", position),
    )
    stream = (residual.astype(jnp.float32) + down).astype(jnp.bfloat16)
    block_stream, block_gain = collect_bits(
        (stream, gain),
        y_positions,
        dev_index,
        lambda current, position: jax.tree.map(
            lambda part, own: part.astype(own.dtype),
            swapped(for_sending(current), "gx", position),
            current,
        ),
    )
    block_values = block_stream.astype(jnp.float32)
    sumsq = jnp.sum(block_values * block_values, axis=0)
    for position in x_positions:
        sumsq = sumsq + swapped(sumsq, "gx", position)
    inv_rms = lax.rsqrt(sumsq / D + 1e-05)
    block_normed = (
        block_values * block_gain.astype(jnp.float32)[:, None] * inv_rms[None, :]
    ).astype(jnp.bfloat16)
    partial_qkv = lax.dot_general(
        tile_qkv, block_normed, (((0,), (0,)), ((), ())), preferred_element_type=jnp.float32
    )
    qkv_order = list(range(x_bits - 1, -1, -1))
    qkv = halve_bits(
        partial_qkv,
        y_bits,
        x_bits,
        qkv_order,
        dev_index,
        lambda current, position: swapped(current, "gx", position),
    )
    return (stream, qkv.astype(jnp.bfloat16))


def ring_position(tile, count):
    odd = lax.rem(tile, 2)
    step = tile // 2
    return (1 - odd) * step + odd * (count - 1 - step)


def ring_tile(position, count):
    back = position // (count // 2)
    return (1 - back) * (2 * position) + back * (2 * (count - 1 - position) + 1)


def fused_kernel(
    xs,
    ys,
    cuts,
    width,
    hidden,
    residual,
    w_down,
    gain,
    w_qkv,
    stream_out,
    qkv_out,
    held,
    res_buf,
    down_buf,
    qkv_buf,
    acc,
    acc_in,
    feats,
    sums,
    pair_sums,
    ring_sums,
    out_msg,
    in_msg,
    own,
    local_sem,
    down_sem,
    qkv_sem,
    ring_send,
    ring_recv,
    acc_send,
    acc_recv,
    feat_send,
    feat_recv,
    psum_send,
    psum_recv,
    rsum_send,
    rsum_recv,
    msg_send,
    msg_recv,
):
    me = lax.axis_index("gx")
    tile, part = me // ys, lax.rem(me, ys)
    place = ring_position(tile, xs)
    rows = hidden.shape[0]
    cut = rows // cuts
    tokens = hidden.shape[1]
    feat = residual.shape[0]
    cols = qkv_out.shape[0]
    half_ring = xs // 2
    half = tokens // 2

    def device_at(x, y):
        return {"gx": x * ys + y}

    def tile_at(direction, distance):
        return ring_tile(lax.rem(place + (2 * direction - 1) * distance + xs, xs), xs)

    ahead = [device_at(tile_at(1, 1), part), device_at(tile_at(0, 1), part)]

    def arrival(direction, item):
        piece = tile_at(direction, item // cuts + 1)
        order = lax.rem(item, cuts)
        return piece, order if direction == 0 else cuts - 1 - order

    def window(piece, chunk):
        return held.at[piece, pl.ds(pl.multiple_of(chunk * cut, cut), cut)]

    def gather_copy(direction, item, piece, chunk, source):
        return pltpu.make_async_remote_copy(
            src_ref=source,
            dst_ref=window(piece, chunk),
            send_sem=ring_send.at[direction, item],
            recv_sem=ring_recv.at[direction, item],
            device_id=ahead[direction],
            device_id_type=MESH,
        )

    def down_copy(slot, piece, chunk):
        start = pl.multiple_of(piece * rows + chunk * cut, cut)
        return pltpu.make_async_copy(
            w_down.at[pl.ds(start, cut)], down_buf.at[slot], down_sem.at[slot]
        )

    def qkv_copy(owner):
        return pltpu.make_async_copy(
            w_qkv.at[:, pl.ds(owner * cols, cols)], qkv_buf.at[owner], qkv_sem.at[owner]
        )

    barrier = pltpu.get_barrier_semaphore()
    for offset in range(1, xs):
        pl.semaphore_signal(
            barrier,
            inc=1,
            device_id=device_at(lax.rem(tile + offset, xs), part),
            device_id_type=MESH,
        )
    for offset in range(1, ys):
        pl.semaphore_signal(
            barrier,
            inc=1,
            device_id=device_at(tile, lax.rem(part + offset, ys)),
            device_id_type=MESH,
        )
    pl.semaphore_wait(barrier, xs - 1 + ys - 1)

    arrivals = cuts * (half_ring - 1) + cuts // 2
    for item in range(cuts):
        for direction in range(2):
            chunk = item if direction == 0 else cuts - 1 - item
            gather_copy(
                direction, item, tile, chunk, hidden.at[pl.ds(chunk * cut, cut)]
            ).start()
    own_copy = pltpu.make_async_copy(hidden, held.at[tile], local_sem.at[0])
    own_copy.start()
    res_copy = pltpu.make_async_copy(residual, res_buf, local_sem.at[1])
    res_copy.start()
    for lane in range(2):
        down_copy(lane, tile, lane).start()
    acc[...] = jnp.zeros_like(acc)
    res_copy.wait()
    acc[part] = res_buf[...].astype(jnp.float32).T
    own_copy.wait()

    def transposed(piece, chunk):
        return held[piece, pl.ds(pl.multiple_of(chunk * cut, cut), cut), :].T

    def add_block(block, base, first, first_slot, second, second_slot):
        for start in range(0, feat, width):
            at = pl.ds(pl.multiple_of(base + start, width), width)
            acc[block, :, start : start + width] += jnp.dot(
                first, down_buf[first_slot, :, at], preferred_element_type=jnp.float32
            ) + jnp.dot(second, down_buf[second_slot, :, at], preferred_element_type=jnp.float32)

    def own_pair(pair, carry):
        slot = lax.rem(pair, 2) * 2
        following = 2 - slot

        @pl.when(pair + 1 < cuts // 2)
        def _():
            for lane in range(2):
                down_copy(following + lane, tile, 2 * pair + 2 + lane).start()

        @pl.when(pair + 1 == cuts // 2)
        def _():
            for lane in range(2):
                down_copy(following + lane, *arrival(lane, 0)).start()

        for lane in range(2):
            down_copy(slot + lane, tile, 2 * pair + lane).wait()
        first, second = transposed(tile, 2 * pair), transposed(tile, 2 * pair + 1)
        for block in range(ys):
            add_block(block, block * feat, first, slot, second, slot + 1)
        return carry

    lax.fori_loop(0, cuts // 2, own_pair, 0)
    for owner in range(xs):
        qkv_copy(owner).start()

    def receive(item, forward):
        for direction in range(2):
            piece, chunk = arrival(direction, item)
            gather_copy(direction, item, piece, chunk, window(piece, chunk)).wait_recv()
            if forward:

                @pl.when(item + cuts < arrivals)
                def _():
                    gather_copy(
                        direction, item + cuts, piece, chunk, window(piece, chunk)
                    ).start()

    def weights_of(item, slot):
        for lane in range(2):
            down_copy(slot + lane, *arrival(lane, item)).wait()

    def ring_pair(item, carry):
        slot = lax.rem(item + cuts // 2, 2) * 2
        following = 2 - slot
        for lane in range(2):
            down_copy(following + lane, *arrival(lane, item + 1)).start()
        receive(item, True)
        weights_of(item, slot)
        first, second = transposed(*arrival(0, item)), transposed(*arrival(1, item))
        for block in range(ys):
            add_block(block, block * feat, first, slot, second, slot + 1)
        return carry

    lax.fori_loop(0, arrivals - 1, ring_pair, 0)

    last = arrivals - 1
    slot = (last + cuts // 2) % 2 * 2
    receive(last, False)
    weights_of(last, slot)
    first, second = transposed(*arrival(0, last)), transposed(*arrival(1, last))
    acc_copies = []
    for offset in range(1, ys):
        other = lax.rem(part + offset, ys)
        add_block(other, other * feat, first, slot, second, slot + 1)
        acc_copies.append(
            pltpu.make_async_remote_copy(
                src_ref=acc.at[other],
                dst_ref=acc_in.at[offset - 1],
                send_sem=acc_send.at[offset - 1],
                recv_sem=acc_recv.at[offset - 1],
                device_id=device_at(tile, other),
                device_id_type=MESH,
            )
        )
        acc_copies[-1].start()
    add_block(part, part * feat, first, slot, second, slot + 1)
    total = acc[part]
    for copy in acc_copies:
        copy.wait_recv()
    for offset in range(1, ys):
        total = total + acc_in[offset - 1]
    values = total.astype(jnp.bfloat16).astype(jnp.float32)
    acc[part] = values
    feats[part] = (values * gain[...].astype(jnp.float32)).astype(jnp.bfloat16)
    feat_copies = []
    for offset in range(1, ys):
        other = lax.rem(part + offset, ys)
        feat_copies.append(
            [
                pltpu.make_async_remote_copy(
                    src_ref=feats.at[sender],
                    dst_ref=feats.at[sender],
                    send_sem=feat_send.at[offset - 1],
                    recv_sem=feat_recv.at[offset - 1],
                    device_id=device_at(tile, other),
                    device_id_type=MESH,
                )
                for sender in (part, lax.rem(part + ys - offset, ys))
            ]
        )
        feat_copies[-1][0].start()

    upright = acc[part].T
    stream_out[...] = upright.astype(jnp.bfloat16)
    sums[...] = jnp.broadcast_to(jnp.sum(upright * upright, axis=0, keepdims=True), sums.shape)
    sum_copies = []
    for offset in range(1, ys):
        sum_copies.append(
            pltpu.make_async_remote_copy(
                src_ref=sums,
                dst_ref=pair_sums.at[offset - 1],
                send_sem=psum_send.at[offset - 1],
                recv_sem=psum_recv.at[offset - 1],
                device_id=device_at(tile, lax.rem(part + offset, ys)),
                device_id_type=MESH,
            )
        )
        sum_copies[-1].start()

    for owner in range(xs):
        qkv_copy(owner).wait()
    for _, incoming in feat_copies:
        incoming.wait_recv()

    def project(owner, start, size):
        result = jnp.dot(
            feats[0, pl.ds(start, size), :],
            qkv_buf[owner, :feat, :],
            preferred_element_type=jnp.float32,
        )
        for block in range(1, ys):
            result = result + jnp.dot(
                feats[block, pl.ds(start, size), :],
                qkv_buf[owner, block * feat : (block + 1) * feat, :],
                preferred_element_type=jnp.float32,
            )
        return result

    def message_copy(direction, index):
        return pltpu.make_async_remote_copy(
            src_ref=out_msg.at[direction, index],
            dst_ref=in_msg.at[direction, index],
            send_sem=msg_send.at[direction, index],
            recv_sem=msg_recv.at[direction, index],
            device_id=ahead[direction],
            device_id_type=MESH,
        )

    def message(index, with_arrived):
        distance = half_ring - (index + 1) // 2
        for direction in range(2):
            odd = lax.rem(index, 2)
            token_half = odd if direction == 0 else 1 - odd
            owner = tile_at(1 - direction, distance)
            value = project(owner, pl.multiple_of(token_half * half, half), half)
            if with_arrived:
                message_copy(direction, index - 2).wait_recv()
                value = value + in_msg[direction, index - 2].astype(jnp.float32)
            out_msg[direction, index] = value.astype(jnp.bfloat16)
            message_copy(direction, index).start()

    messages = 2 * half_ring - 1

    def first_messages(index, carry):
        message(index, False)
        return carry

    def later_messages(index, carry):
        message(index, True)
        return carry

    lax.fori_loop(0, 2, first_messages, 0)

    for copy in sum_copies:
        copy.wait_recv()
    tile_sums = sums[...]
    for offset in range(1, ys):
        tile_sums = tile_sums + pair_sums[offset - 1]
    ring_sums[0] = tile_sums
    for offset in range(1, xs):
        sum_copies.append(
            pltpu.make_async_remote_copy(
                src_ref=ring_sums.at[0],
                dst_ref=ring_sums.at[offset],
                send_sem=rsum_send.at[offset - 1],
                recv_sem=rsum_recv.at[offset - 1],
                device_id=device_at(lax.rem(tile + offset, xs), part),
                device_id_type=MESH,
            )
        )
        sum_copies[-1].start()

    lax.fori_loop(2, messages, later_messages, 0)

    own[...] = project(tile, 0, tokens)
    for copy in sum_copies[ys - 1 :]:
        copy.wait_recv()
    all_sums = ring_sums[0]
    for offset in range(1, xs):
        all_sums = all_sums + ring_sums[offset]
    inv_rms = lax.rsqrt(all_sums[0:1] / (feat * xs * ys) + 1e-05)
    for index in range(messages - 2, messages):
        for direction in range(2):
            token_half = index % 2 if direction == 0 else 1 - index % 2
            message_copy(direction, index).wait_recv()
            own[token_half * half : (token_half + 1) * half, :] += in_msg[
                direction, index
            ].astype(jnp.float32)
    qkv_out[...] = (own[...].T * inv_rms).astype(jnp.bfloat16)

    for direction in range(2):
        for item in range(arrivals):
            gather_copy(direction, item, tile, 0, window(tile, 0)).wait_send()
        for index in range(messages):
            message_copy(direction, index).wait_send()
    for copy in acc_copies + sum_copies:
        copy.wait_send()
    for outgoing, _ in feat_copies:
        outgoing.wait_send()


def fused(hidden, residual, w_down, gain, w_qkv):
    gx = lax.axis_size("gx")
    xs, ys = XS, gx // XS
    rows, tokens = hidden.shape
    feat = residual.shape[0]
    cols = w_qkv.shape[2] // xs
    cuts = next(c for c in (4, 2) if rows % (16 * c) == 0)
    width = next(w for w in (512, 256, 128) if feat % w == 0)
    arrivals = cuts * (xs // 2 - 1) + cuts // 2
    messages = xs - 1
    others = max(ys - 1, 1)
    dma = pltpu.SemaphoreType.DMA
    flops = 2 * tokens * (w_down.shape[1] * w_down.shape[2] + w_qkv.shape[1] * w_qkv.shape[2])
    return pl.pallas_call(
        functools.partial(fused_kernel, xs, ys, cuts, width),
        out_shape=(
            jax.ShapeDtypeStruct((feat, tokens), jnp.bfloat16),
            jax.ShapeDtypeStruct((cols, tokens), jnp.bfloat16),
        ),
        in_specs=[
            pl.BlockSpec(memory_space=pl.ANY),
            pl.BlockSpec(memory_space=pl.ANY),
            pl.BlockSpec(memory_space=pl.ANY),
            pl.BlockSpec(memory_space=pltpu.VMEM),
            pl.BlockSpec(memory_space=pl.ANY),
        ],
        out_specs=(
            pl.BlockSpec(memory_space=pltpu.VMEM),
            pl.BlockSpec(memory_space=pltpu.VMEM),
        ),
        scratch_shapes=[
            pltpu.VMEM((xs, rows, tokens), jnp.bfloat16),
            pltpu.VMEM((feat, tokens), jnp.bfloat16),
            pltpu.VMEM((4, rows // cuts, ys * feat), jnp.bfloat16),
            pltpu.VMEM((xs, ys * feat, cols), jnp.bfloat16),
            pltpu.VMEM((ys, tokens, feat), jnp.float32),
            pltpu.VMEM((others, tokens, feat), jnp.float32),
            pltpu.VMEM((ys, tokens, feat), jnp.bfloat16),
            pltpu.VMEM((8, tokens), jnp.float32),
            pltpu.VMEM((others, 8, tokens), jnp.float32),
            pltpu.VMEM((xs, 8, tokens), jnp.float32),
            pltpu.VMEM((2, messages, tokens // 2, cols), jnp.bfloat16),
            pltpu.VMEM((2, messages, tokens // 2, cols), jnp.bfloat16),
            pltpu.VMEM((tokens, cols), jnp.float32),
            dma((2,)),
            dma((4,)),
            dma((xs,)),
            dma((2, arrivals)),
            dma((2, arrivals)),
            dma((others,)),
            dma((others,)),
            dma((others,)),
            dma((others,)),
            dma((others,)),
            dma((others,)),
            dma((xs - 1,)),
            dma((xs - 1,)),
            dma((2, messages)),
            dma((2, messages)),
        ],
        compiler_params=pltpu.CompilerParams(
            collective_id=0, has_side_effects=True, vmem_limit_bytes=66 * 10**6
        ),
        cost_estimate=pl.CostEstimate(
            flops=flops,
            bytes_accessed=2 * (w_down.size + w_qkv.size),
            transcendentals=0,
        ),
    )(hidden, residual, w_down[0], gain[None, :], w_qkv[0])


def on_device(hidden, residual, w_down, gain, w_qkv):
    cols = w_qkv.shape[2] // XS
    aligned = (
        hidden.shape[0] % 32 == 0
        and hidden.shape[1] % 32 == 0
        and residual.shape[0] % 128 == 0
        and cols % 128 == 0
    )
    step = fused if aligned else permuted
    return step(hidden, residual, w_down, gain, w_qkv)


def solution(mesh):
    placed = (
        P("gx", "groups"),
        P("gx", "groups"),
        P("gx", None, None),
        P("gx"),
        P("gx", None, None),
    )
    return jax.shard_map(
        on_device,
        mesh=mesh,
        in_specs=placed,
        out_specs=(P("gx", "groups"), P("gx", "groups")),
        check_vma=False,
    )
```

```python
import functools

import jax
import jax.numpy as jnp
from jax import lax
from jax.experimental import pallas as pl
from jax.experimental.pallas import tpu as pltpu
from jax.sharding import PartitionSpec as P

D = 16384
XS = 8
MESH = pl.DeviceIdType.MESH


def swapped(block, axis, stride):
    count = lax.axis_size(axis)
    route = []
    for low in range(count):
        high = low | 1 << stride
        if high != low and high < count:
            route += [(low, high), (high, low)]
    return lax.ppermute(block, axis, route)


def for_sending(value):
    return jax.tree.map(lambda a: a.astype(jnp.bfloat16) if a.dtype == jnp.float32 else a, value)


def bit_of(dev_index, position):
    return dev_index // 2**position % 2


def collect_bits(current, positions, dev_index, send_fn):
    for position in positions:
        received = send_fn(current, position)
        high_bit = bit_of(dev_index, position) == 1
        current = jax.tree.map(
            lambda own_part, their_part: jnp.where(
                high_bit,
                jnp.concatenate([their_part, own_part], 0),
                jnp.concatenate([own_part, their_part], 0),
            ),
            current,
            received,
        )
    return current


def halve_bits(partial_value, first_bit, bit_count, bit_order, dev_index, send_fn):
    trailing = partial_value.shape[1:]
    shaped = partial_value.reshape(
        (2,) * bit_count + (partial_value.shape[0] // 2**bit_count,) + trailing
    )
    remaining = list(range(bit_count - 1, -1, -1))
    for relative in bit_order:
        axis_pos = sum([1 for other in remaining if other > relative])
        high_bit = bit_of(dev_index, first_bit + relative)
        retained = lax.dynamic_index_in_dim(shaped, high_bit, axis_pos, keepdims=False)
        outgoing = lax.dynamic_index_in_dim(shaped, 1 - high_bit, axis_pos, keepdims=False)
        shaped = retained + send_fn(outgoing, first_bit + relative)
        remaining = [other for other in remaining if other != relative]
    return shaped


def permuted(hidden, residual, w_down, gain, w_qkv):
    dev_index = lax.axis_index("gx")
    y_bits = (lax.axis_size("gx") // XS).bit_length() - 1
    x_bits = XS.bit_length() - 1
    x_positions = list(range(y_bits, y_bits + x_bits))
    y_positions = list(range(y_bits))
    tile_down = w_down[0]
    tile_qkv = w_qkv[0]
    gathered = collect_bits(
        hidden, x_positions, dev_index, lambda current, position: swapped(current, "gx", position)
    )
    partial_down = lax.dot_general(
        tile_down, gathered, (((0,), (0,)), ((), ())), preferred_element_type=jnp.float32
    )
    down_order = list(range(y_bits - 1, -1, -1))
    down = halve_bits(
        partial_down,
        0,
        y_bits,
        down_order,
        dev_index,
        lambda current, position: swapped(current, "gx", position),
    )
    stream = (residual.astype(jnp.float32) + down).astype(jnp.bfloat16)
    block_stream, block_gain = collect_bits(
        (stream, gain),
        y_positions,
        dev_index,
        lambda current, position: jax.tree.map(
            lambda part, own: part.astype(own.dtype),
            swapped(for_sending(current), "gx", position),
            current,
        ),
    )
    block_values = block_stream.astype(jnp.float32)
    sumsq = jnp.sum(block_values * block_values, axis=0)
    for position in x_positions:
        sumsq = sumsq + swapped(sumsq, "gx", position)
    inv_rms = lax.rsqrt(sumsq / D + 1e-05)
    block_normed = (
        block_values * block_gain.astype(jnp.float32)[:, None] * inv_rms[None, :]
    ).astype(jnp.bfloat16)
    partial_qkv = lax.dot_general(
        tile_qkv, block_normed, (((0,), (0,)), ((), ())), preferred_element_type=jnp.float32
    )
    qkv_order = list(range(x_bits - 1, -1, -1))
    qkv = halve_bits(
        partial_qkv,
        y_bits,
        x_bits,
        qkv_order,
        dev_index,
        lambda current, position: swapped(current, "gx", position),
    )
    return (stream, qkv.astype(jnp.bfloat16))


def ring_position(tile, count):
    odd = lax.rem(tile, 2)
    step = tile // 2
    return (1 - odd) * step + odd * (count - 1 - step)


def ring_tile(position, count):
    back = position // (count // 2)
    return (1 - back) * (2 * position) + back * (2 * (count - 1 - position) + 1)


def fused_kernel(
    xs,
    ys,
    cuts,
    width,
    hidden,
    residual,
    w_down,
    gain,
    w_qkv,
    stream_out,
    qkv_out,
    held,
    res_buf,
    down_buf,
    qkv_buf,
    acc,
    acc_in,
    feats,
    sums,
    pair_sums,
    ring_sums,
    out_msg,
    in_msg,
    own,
    local_sem,
    down_sem,
    qkv_sem,
    ring_send,
    ring_recv,
    acc_send,
    acc_recv,
    feat_send,
    feat_recv,
    psum_send,
    psum_recv,
    rsum_send,
    rsum_recv,
    msg_send,
    msg_recv,
):
    me = lax.axis_index("gx")
    tile, part = me // ys, lax.rem(me, ys)
    place = ring_position(tile, xs)
    rows = hidden.shape[0]
    cut = rows // cuts
    tokens = hidden.shape[1]
    feat = residual.shape[0]
    cols = qkv_out.shape[0]
    half_ring = xs // 2
    half = tokens // 2

    def device_at(x, y):
        return {"gx": x * ys + y}

    def tile_at(direction, distance):
        return ring_tile(lax.rem(place + (2 * direction - 1) * distance + xs, xs), xs)

    ahead = [device_at(tile_at(1, 1), part), device_at(tile_at(0, 1), part)]

    def arrival(direction, item):
        piece = tile_at(direction, item // cuts + 1)
        order = lax.rem(item, cuts)
        return piece, order if direction == 0 else cuts - 1 - order

    def window(piece, chunk):
        return held.at[piece, pl.ds(pl.multiple_of(chunk * cut, cut), cut)]

    def gather_copy(direction, item, piece, chunk, source):
        return pltpu.make_async_remote_copy(
            src_ref=source,
            dst_ref=window(piece, chunk),
            send_sem=ring_send.at[direction, item],
            recv_sem=ring_recv.at[direction, item],
            device_id=ahead[direction],
            device_id_type=MESH,
        )

    def down_copy(slot, piece, chunk):
        start = pl.multiple_of(piece * rows + chunk * cut, cut)
        return pltpu.make_async_copy(
            w_down.at[pl.ds(start, cut)], down_buf.at[slot], down_sem.at[slot]
        )

    def qkv_copy(owner):
        return pltpu.make_async_copy(
            w_qkv.at[:, pl.ds(owner * cols, cols)], qkv_buf.at[owner], qkv_sem.at[owner]
        )

    barrier = pltpu.get_barrier_semaphore()
    for offset in range(1, xs):
        pl.semaphore_signal(
            barrier,
            inc=1,
            device_id=device_at(lax.rem(tile + offset, xs), part),
            device_id_type=MESH,
        )
    for offset in range(1, ys):
        pl.semaphore_signal(
            barrier,
            inc=1,
            device_id=device_at(tile, lax.rem(part + offset, ys)),
            device_id_type=MESH,
        )
    pl.semaphore_wait(barrier, xs - 1 + ys - 1)

    arrivals = cuts * (half_ring - 1) + cuts // 2


    def send_own(direction, item):
        chunk = item if direction == 0 else cuts - 1 - item
        start = pl.multiple_of(chunk * cut, cut)
        gather_copy(direction, item, tile, chunk, hidden.at[pl.ds(start, cut)]).start()

    for item in range(2):
        for direction in range(2):
            send_own(direction, item)
    own_copy = pltpu.make_async_copy(hidden, held.at[tile], local_sem.at[0])
    own_copy.start()
    res_copy = pltpu.make_async_copy(residual, res_buf, local_sem.at[1])
    res_copy.start()
    for lane in range(2):
        down_copy(lane, tile, lane).start()
    acc[...] = jnp.zeros_like(acc)
    res_copy.wait()
    acc[part] = res_buf[...].astype(jnp.float32).T
    own_copy.wait()

    def transposed(piece, chunk):
        return held[piece, pl.ds(pl.multiple_of(chunk * cut, cut), cut), :].T

    def add_block(block, base, first, first_slot, second, second_slot):
        for start in range(0, feat, width):
            at = pl.ds(pl.multiple_of(base + start, width), width)
            acc[block, :, start : start + width] += jnp.dot(
                first, down_buf[first_slot, :, at], preferred_element_type=jnp.float32
            ) + jnp.dot(second, down_buf[second_slot, :, at], preferred_element_type=jnp.float32)

    def own_pair(pair, carry):
        slot = lax.rem(pair, 2) * 2
        following = 2 - slot

        @pl.when(pair + 1 < cuts // 2)
        def _():
            for lane in range(2):
                down_copy(following + lane, tile, 2 * pair + 2 + lane).start()

        @pl.when(pair + 1 == cuts // 2)
        def _():
            for lane in range(2):
                down_copy(following + lane, *arrival(lane, 0)).start()

        for lane in range(2):
            down_copy(slot + lane, tile, 2 * pair + lane).wait()
        first, second = transposed(tile, 2 * pair), transposed(tile, 2 * pair + 1)
        for block in range(ys):
            add_block(block, block * feat, first, slot, second, slot + 1)
        return carry

    lax.fori_loop(0, cuts // 2, own_pair, 0)
    for owner in range(xs):
        qkv_copy(owner).start()

    def receive(item, forward):
        for direction in range(2):
            piece, chunk = arrival(direction, item)
            gather_copy(direction, item, piece, chunk, window(piece, chunk)).wait_recv()
            if forward:

                @pl.when(item + 2 < cuts)
                def _():
                    send_own(direction, item + 2)

                @pl.when(jnp.logical_and(item + 2 >= cuts, item + 2 < arrivals))
                def _():
                    piece, chunk = arrival(direction, item + 2 - cuts)
                    gather_copy(
                        direction, item + 2, piece, chunk, window(piece, chunk)
                    ).start()

    def weights_of(item, slot):
        for lane in range(2):
            down_copy(slot + lane, *arrival(lane, item)).wait()

    def ring_pair(item, carry):
        slot = lax.rem(item + cuts // 2, 2) * 2
        following = 2 - slot
        for lane in range(2):
            down_copy(following + lane, *arrival(lane, item + 1)).start()
        receive(item, True)
        weights_of(item, slot)
        first, second = transposed(*arrival(0, item)), transposed(*arrival(1, item))
        for block in range(ys):
            add_block(block, block * feat, first, slot, second, slot + 1)
        return carry

    lax.fori_loop(0, arrivals - 1, ring_pair, 0)

    last = arrivals - 1
    slot = (last + cuts // 2) % 2 * 2
    receive(last, False)
    weights_of(last, slot)
    first, second = transposed(*arrival(0, last)), transposed(*arrival(1, last))
    acc_copies = []
    for offset in range(1, ys):
        other = lax.rem(part + offset, ys)
        add_block(other, other * feat, first, slot, second, slot + 1)
        for side in range(2):
            acc_copies.append(
                pltpu.make_async_remote_copy(
                    src_ref=acc.at[other, pl.ds(side * half, half)],
                    dst_ref=acc_in.at[offset - 1, pl.ds(side * half, half)],
                    send_sem=acc_send.at[offset - 1, side],
                    recv_sem=acc_recv.at[offset - 1, side],
                    device_id=device_at(tile, other),
                    device_id_type=MESH,
                )
            )
            acc_copies[-1].start()
    add_block(part, part * feat, first, slot, second, slot + 1)

    def feat_copy(offset, side, sender):
        return pltpu.make_async_remote_copy(
            src_ref=feats.at[sender, pl.ds(side * half, half)],
            dst_ref=feats.at[sender, pl.ds(side * half, half)],
            send_sem=feat_send.at[offset - 1, side],
            recv_sem=feat_recv.at[offset - 1, side],
            device_id=device_at(tile, lax.rem(part + offset, ys)),
            device_id_type=MESH,
        )

    for side in range(2):
        span = slice(side * half, (side + 1) * half)
        total = acc[part, span, :]
        for offset in range(1, ys):
            acc_copies[2 * (offset - 1) + side].wait_recv()
            total = total + acc_in[offset - 1, span, :]
        values = total.astype(jnp.bfloat16).astype(jnp.float32)
        acc[part, span, :] = values
        feats[part, span, :] = (values * gain[...].astype(jnp.float32)[None, :]).astype(jnp.bfloat16)
        for offset in range(1, ys):
            feat_copy(offset, side, part).start()

    def wait_feats(side):
        for offset in range(1, ys):
            feat_copy(offset, side, lax.rem(part + ys - offset, ys)).wait_recv()

    def project(owner, start, size):
        result = jnp.dot(
            feats[0, pl.ds(start, size), :],
            qkv_buf[owner, :feat, :],
            preferred_element_type=jnp.float32,
        )
        for block in range(1, ys):
            result = result + jnp.dot(
                feats[block, pl.ds(start, size), :],
                qkv_buf[owner, block * feat : (block + 1) * feat, :],
                preferred_element_type=jnp.float32,
            )
        return result

    def message_copy(direction, index):
        return pltpu.make_async_remote_copy(
            src_ref=out_msg.at[direction, index],
            dst_ref=in_msg.at[direction, index],
            send_sem=msg_send.at[direction, index],
            recv_sem=msg_recv.at[direction, index],
            device_id=ahead[direction],
            device_id_type=MESH,
        )

    def message(index, with_arrived, first=False):
        distance = half_ring - (index + 1) // 2
        for direction in range(2):
            if first:
                wait_feats(direction)
            odd = lax.rem(index, 2)
            token_half = odd if direction == 0 else 1 - odd
            owner = tile_at(1 - direction, distance)
            value = project(owner, pl.multiple_of(token_half * half, half), half)
            if with_arrived:
                message_copy(direction, index - 2).wait_recv()
                value = value + in_msg[direction, index - 2].astype(jnp.float32)
            out_msg[direction, index] = value.astype(jnp.bfloat16)
            message_copy(direction, index).start()

    messages = 2 * half_ring - 1

    def later_messages(index, carry):
        message(index, True)
        return carry

    for owner in range(xs):
        qkv_copy(owner).wait()
    message(0, False, True)
    message(1, False)

    upright = acc[part].T
    stream_out[...] = upright.astype(jnp.bfloat16)
    sums[...] = jnp.broadcast_to(jnp.sum(upright * upright, axis=0, keepdims=True), sums.shape)
    sum_copies = []
    for offset in range(1, ys):
        sum_copies.append(
            pltpu.make_async_remote_copy(
                src_ref=sums,
                dst_ref=pair_sums.at[offset - 1],
                send_sem=psum_send.at[offset - 1],
                recv_sem=psum_recv.at[offset - 1],
                device_id=device_at(tile, lax.rem(part + offset, ys)),
                device_id_type=MESH,
            )
        )
        sum_copies[-1].start()
    lax.fori_loop(2, messages - 3, later_messages, 0)

    for copy in sum_copies:
        copy.wait_recv()
    tile_sums = sums[...]
    for offset in range(1, ys):
        tile_sums = tile_sums + pair_sums[offset - 1]
    ring_sums[0] = tile_sums
    for offset in range(1, xs):
        sum_copies.append(
            pltpu.make_async_remote_copy(
                src_ref=ring_sums.at[0],
                dst_ref=ring_sums.at[offset],
                send_sem=rsum_send.at[offset - 1],
                recv_sem=rsum_recv.at[offset - 1],
                device_id=device_at(lax.rem(tile + offset, xs), part),
                device_id_type=MESH,
            )
        )
        sum_copies[-1].start()

    lax.fori_loop(messages - 3, messages, later_messages, 0)

    own[...] = project(tile, 0, tokens)
    for copy in sum_copies[ys - 1 :]:
        copy.wait_recv()
    all_sums = ring_sums[0]
    for offset in range(1, xs):
        all_sums = all_sums + ring_sums[offset]
    inv_rms = lax.rsqrt(all_sums[0:1] / (feat * xs * ys) + 1e-05)
    for index in range(messages - 2, messages):
        for direction in range(2):
            token_half = index % 2 if direction == 0 else 1 - index % 2
            message_copy(direction, index).wait_recv()
            own[token_half * half : (token_half + 1) * half, :] += in_msg[
                direction, index
            ].astype(jnp.float32)
    qkv_out[...] = (own[...].T * inv_rms).astype(jnp.bfloat16)

    for direction in range(2):
        for item in range(arrivals):
            gather_copy(direction, item, tile, 0, window(tile, 0)).wait_send()
        for index in range(messages):
            message_copy(direction, index).wait_send()
    for copy in acc_copies + sum_copies:
        copy.wait_send()
    for offset in range(1, ys):
        for side in range(2):
            feat_copy(offset, side, part).wait_send()


def fused(hidden, residual, w_down, gain, w_qkv):
    gx = lax.axis_size("gx")
    xs, ys = XS, gx // XS
    rows, tokens = hidden.shape
    feat = residual.shape[0]
    cols = w_qkv.shape[2] // xs
    cuts = next(c for c in (6, 4, 2) if rows % (16 * c) == 0)
    width = next(w for w in (512, 256, 128) if feat % w == 0)
    arrivals = cuts * (xs // 2 - 1) + cuts // 2
    messages = xs - 1
    others = max(ys - 1, 1)
    dma = pltpu.SemaphoreType.DMA
    flops = 2 * tokens * (w_down.shape[1] * w_down.shape[2] + w_qkv.shape[1] * w_qkv.shape[2])
    return pl.pallas_call(
        functools.partial(fused_kernel, xs, ys, cuts, width),
        out_shape=(
            jax.ShapeDtypeStruct((feat, tokens), jnp.bfloat16),
            jax.ShapeDtypeStruct((cols, tokens), jnp.bfloat16),
        ),
        in_specs=[
            pl.BlockSpec(memory_space=pl.ANY),
            pl.BlockSpec(memory_space=pl.ANY),
            pl.BlockSpec(memory_space=pl.ANY),
            pl.BlockSpec(memory_space=pltpu.VMEM),
            pl.BlockSpec(memory_space=pl.ANY),
        ],
        out_specs=(
            pl.BlockSpec(memory_space=pltpu.VMEM),
            pl.BlockSpec(memory_space=pltpu.VMEM),
        ),
        scratch_shapes=[
            pltpu.VMEM((xs, rows, tokens), jnp.bfloat16),
            pltpu.VMEM((feat, tokens), jnp.bfloat16),
            pltpu.VMEM((4, rows // cuts, ys * feat), jnp.bfloat16),
            pltpu.VMEM((xs, ys * feat, cols), jnp.bfloat16),
            pltpu.VMEM((ys, tokens, feat), jnp.float32),
            pltpu.VMEM((others, tokens, feat), jnp.float32),
            pltpu.VMEM((ys, tokens, feat), jnp.bfloat16),
            pltpu.VMEM((8, tokens), jnp.float32),
            pltpu.VMEM((others, 8, tokens), jnp.float32),
            pltpu.VMEM((xs, 8, tokens), jnp.float32),
            pltpu.VMEM((2, messages, tokens // 2, cols), jnp.bfloat16),
            pltpu.VMEM((2, messages, tokens // 2, cols), jnp.bfloat16),
            pltpu.VMEM((tokens, cols), jnp.float32),
            dma((2,)),
            dma((4,)),
            dma((xs,)),
            dma((2, arrivals)),
            dma((2, arrivals)),
            dma((others, 2)),
            dma((others, 2)),
            dma((others, 2)),
            dma((others, 2)),
            dma((others,)),
            dma((others,)),
            dma((xs - 1,)),
            dma((xs - 1,)),
            dma((2, messages)),
            dma((2, messages)),
        ],
        compiler_params=pltpu.CompilerParams(
            collective_id=0, has_side_effects=True, vmem_limit_bytes=66 * 10**6
        ),
        cost_estimate=pl.CostEstimate(
            flops=flops,
            bytes_accessed=2 * (w_down.size + w_qkv.size),
            transcendentals=0,
        ),
    )(hidden, residual, w_down[0], gain, w_qkv[0])


def on_device(hidden, residual, w_down, gain, w_qkv):
    cols = w_qkv.shape[2] // XS
    aligned = (
        hidden.shape[0] % 32 == 0
        and hidden.shape[1] % 32 == 0
        and residual.shape[0] % 128 == 0
        and cols % 128 == 0
    )
    step = fused if aligned else permuted
    return step(hidden, residual, w_down, gain, w_qkv)


def solution(mesh):
    placed = (
        P("gx", "groups"),
        P("gx", "groups"),
        P("gx", None, None),
        P("gx"),
        P("gx", None, None),
    )
    return jax.shard_map(
        on_device,
        mesh=mesh,
        in_specs=placed,
        out_specs=(P("gx", "groups"), P("gx", "groups")),
        check_vma=False,
    )
```

```python
import functools

import jax
import jax.numpy as jnp
from jax import lax
from jax.experimental import pallas as pl
from jax.experimental.pallas import tpu as pltpu
from jax.sharding import PartitionSpec as P

D = 16384
XS = 8
MESH = pl.DeviceIdType.MESH


def swapped(block, axis, stride):
    count = lax.axis_size(axis)
    route = []
    for low in range(count):
        high = low | 1 << stride
        if high != low and high < count:
            route += [(low, high), (high, low)]
    return lax.ppermute(block, axis, route)


def for_sending(value):
    return jax.tree.map(lambda a: a.astype(jnp.bfloat16) if a.dtype == jnp.float32 else a, value)


def bit_of(dev_index, position):
    return dev_index // 2**position % 2


def collect_bits(current, positions, dev_index, send_fn):
    for position in positions:
        received = send_fn(current, position)
        high_bit = bit_of(dev_index, position) == 1
        current = jax.tree.map(
            lambda own_part, their_part: jnp.where(
                high_bit,
                jnp.concatenate([their_part, own_part], 0),
                jnp.concatenate([own_part, their_part], 0),
            ),
            current,
            received,
        )
    return current


def halve_bits(partial_value, first_bit, bit_count, bit_order, dev_index, send_fn):
    trailing = partial_value.shape[1:]
    shaped = partial_value.reshape(
        (2,) * bit_count + (partial_value.shape[0] // 2**bit_count,) + trailing
    )
    remaining = list(range(bit_count - 1, -1, -1))
    for relative in bit_order:
        axis_pos = sum([1 for other in remaining if other > relative])
        high_bit = bit_of(dev_index, first_bit + relative)
        retained = lax.dynamic_index_in_dim(shaped, high_bit, axis_pos, keepdims=False)
        outgoing = lax.dynamic_index_in_dim(shaped, 1 - high_bit, axis_pos, keepdims=False)
        shaped = retained + send_fn(outgoing, first_bit + relative)
        remaining = [other for other in remaining if other != relative]
    return shaped


def permuted(hidden, residual, w_down, gain, w_qkv):
    dev_index = lax.axis_index("gx")
    y_bits = (lax.axis_size("gx") // XS).bit_length() - 1
    x_bits = XS.bit_length() - 1
    x_positions = list(range(y_bits, y_bits + x_bits))
    y_positions = list(range(y_bits))
    tile_down = w_down[0]
    tile_qkv = w_qkv[0]
    gathered = collect_bits(
        hidden, x_positions, dev_index, lambda current, position: swapped(current, "gx", position)
    )
    partial_down = lax.dot_general(
        tile_down, gathered, (((0,), (0,)), ((), ())), preferred_element_type=jnp.float32
    )
    down_order = list(range(y_bits - 1, -1, -1))
    down = halve_bits(
        partial_down,
        0,
        y_bits,
        down_order,
        dev_index,
        lambda current, position: swapped(current, "gx", position),
    )
    stream = (residual.astype(jnp.float32) + down).astype(jnp.bfloat16)
    block_stream, block_gain = collect_bits(
        (stream, gain),
        y_positions,
        dev_index,
        lambda current, position: jax.tree.map(
            lambda part, own: part.astype(own.dtype),
            swapped(for_sending(current), "gx", position),
            current,
        ),
    )
    block_values = block_stream.astype(jnp.float32)
    sumsq = jnp.sum(block_values * block_values, axis=0)
    for position in x_positions:
        sumsq = sumsq + swapped(sumsq, "gx", position)
    inv_rms = lax.rsqrt(sumsq / D + 1e-05)
    block_normed = (
        block_values * block_gain.astype(jnp.float32)[:, None] * inv_rms[None, :]
    ).astype(jnp.bfloat16)
    partial_qkv = lax.dot_general(
        tile_qkv, block_normed, (((0,), (0,)), ((), ())), preferred_element_type=jnp.float32
    )
    qkv_order = list(range(x_bits - 1, -1, -1))
    qkv = halve_bits(
        partial_qkv,
        y_bits,
        x_bits,
        qkv_order,
        dev_index,
        lambda current, position: swapped(current, "gx", position),
    )
    return (stream, qkv.astype(jnp.bfloat16))


def ring_position(tile, count):
    odd = lax.rem(tile, 2)
    step = tile // 2
    return (1 - odd) * step + odd * (count - 1 - step)


def ring_tile(position, count):
    back = position // (count // 2)
    return (1 - back) * (2 * position) + back * (2 * (count - 1 - position) + 1)


def fused_kernel(
    xs,
    ys,
    cuts,
    width,
    hidden,
    residual,
    w_down,
    gain,
    w_qkv,
    stream_out,
    qkv_out,
    held,
    res_buf,
    down_buf,
    qkv_buf,
    acc,
    acc_in,
    feats,
    sums,
    pair_sums,
    ring_sums,
    out_msg,
    in_msg,
    own,
    local_sem,
    down_sem,
    qkv_sem,
    ring_send,
    ring_recv,
    acc_send,
    acc_recv,
    feat_send,
    feat_recv,
    psum_send,
    psum_recv,
    rsum_send,
    rsum_recv,
    msg_send,
    msg_recv,
):
    me = lax.axis_index("gx")
    tile, part = me // ys, lax.rem(me, ys)
    place = ring_position(tile, xs)
    rows = hidden.shape[0]
    cut = rows // cuts
    tokens = hidden.shape[1]
    feat = residual.shape[0]
    cols = qkv_out.shape[0]
    half_ring = xs // 2
    half = tokens // 2

    def device_at(x, y):
        return {"gx": x * ys + y}

    def tile_at(direction, distance):
        return ring_tile(lax.rem(place + (2 * direction - 1) * distance + xs, xs), xs)

    ahead = [device_at(tile_at(1, 1), part), device_at(tile_at(0, 1), part)]

    def arrival(direction, item):
        piece = tile_at(direction, item // cuts + 1)
        order = lax.rem(item, cuts)
        return piece, order if direction == 0 else cuts - 1 - order

    def window(piece, chunk):
        return held.at[piece, pl.ds(pl.multiple_of(chunk * cut, cut), cut)]

    def gather_copy(direction, item, piece, chunk, source):
        return pltpu.make_async_remote_copy(
            src_ref=source,
            dst_ref=window(piece, chunk),
            send_sem=ring_send.at[direction, item],
            recv_sem=ring_recv.at[direction, item],
            device_id=ahead[direction],
            device_id_type=MESH,
        )

    def down_copy(slot, piece, chunk):
        start = pl.multiple_of(piece * rows + chunk * cut, cut)
        return pltpu.make_async_copy(
            w_down.at[pl.ds(start, cut)], down_buf.at[slot], down_sem.at[slot]
        )

    def qkv_copy(owner):
        return pltpu.make_async_copy(
            w_qkv.at[:, pl.ds(owner * cols, cols)], qkv_buf.at[owner], qkv_sem.at[owner]
        )

    barrier = pltpu.get_barrier_semaphore()
    for offset in range(1, xs):
        pl.semaphore_signal(
            barrier,
            inc=1,
            device_id=device_at(lax.rem(tile + offset, xs), part),
            device_id_type=MESH,
        )
    for offset in range(1, ys):
        pl.semaphore_signal(
            barrier,
            inc=1,
            device_id=device_at(tile, lax.rem(part + offset, ys)),
            device_id_type=MESH,
        )
    pl.semaphore_wait(barrier, xs - 1 + ys - 1)

    arrivals = cuts * (half_ring - 1) + cuts // 2


    def send_own(direction, item):
        chunk = item if direction == 0 else cuts - 1 - item
        start = pl.multiple_of(chunk * cut, cut)
        gather_copy(direction, item, tile, chunk, hidden.at[pl.ds(start, cut)]).start()

    for item in range(2):
        for direction in range(2):
            send_own(direction, item)
    own_copy = pltpu.make_async_copy(hidden, held.at[tile], local_sem.at[0])
    own_copy.start()
    res_copy = pltpu.make_async_copy(residual, res_buf, local_sem.at[1])
    res_copy.start()
    for lane in range(2):
        down_copy(lane, tile, lane).start()
    acc[...] = jnp.zeros_like(acc)
    res_copy.wait()
    acc[part] = res_buf[...].astype(jnp.float32).T
    own_copy.wait()

    def transposed(piece, chunk):
        return held[piece, pl.ds(pl.multiple_of(chunk * cut, cut), cut), :].T

    def add_block(block, base, first, first_slot, second, second_slot):
        for start in range(0, feat, width):
            at = pl.ds(pl.multiple_of(base + start, width), width)
            acc[block, :, start : start + width] += jnp.dot(
                first, down_buf[first_slot, :, at], preferred_element_type=jnp.float32
            ) + jnp.dot(second, down_buf[second_slot, :, at], preferred_element_type=jnp.float32)

    def own_pair(pair, carry):
        slot = lax.rem(pair, 2) * 2
        following = 2 - slot

        @pl.when(pair + 1 < cuts // 2)
        def _():
            for lane in range(2):
                down_copy(following + lane, tile, 2 * pair + 2 + lane).start()

        @pl.when(pair + 1 == cuts // 2)
        def _():
            for lane in range(2):
                down_copy(following + lane, *arrival(lane, 0)).start()

        for lane in range(2):
            down_copy(slot + lane, tile, 2 * pair + lane).wait()
        first, second = transposed(tile, 2 * pair), transposed(tile, 2 * pair + 1)
        for block in range(ys):
            add_block(block, block * feat, first, slot, second, slot + 1)
        return carry

    lax.fori_loop(0, cuts // 2, own_pair, 0)
    for owner in range(xs):
        qkv_copy(owner).start()

    def receive(item, forward):
        for direction in range(2):
            piece, chunk = arrival(direction, item)
            gather_copy(direction, item, piece, chunk, window(piece, chunk)).wait_recv()
            if forward:

                @pl.when(item + 2 < cuts)
                def _():
                    send_own(direction, item + 2)

                @pl.when(jnp.logical_and(item + 2 >= cuts, item + 2 < arrivals))
                def _():
                    piece, chunk = arrival(direction, item + 2 - cuts)
                    gather_copy(
                        direction, item + 2, piece, chunk, window(piece, chunk)
                    ).start()

    def weights_of(item, slot):
        for lane in range(2):
            down_copy(slot + lane, *arrival(lane, item)).wait()

    def ring_pair(item, carry):
        slot = lax.rem(item + cuts // 2, 2) * 2
        following = 2 - slot
        for lane in range(2):
            down_copy(following + lane, *arrival(lane, item + 1)).start()
        receive(item, True)
        weights_of(item, slot)
        first, second = transposed(*arrival(0, item)), transposed(*arrival(1, item))
        for block in range(ys):
            add_block(block, block * feat, first, slot, second, slot + 1)
        return carry

    lax.fori_loop(0, arrivals - 1, ring_pair, 0)

    last = arrivals - 1
    slot = (last + cuts // 2) % 2 * 2
    receive(last, False)
    weights_of(last, slot)
    first, second = transposed(*arrival(0, last)), transposed(*arrival(1, last))
    acc_copies = []
    for offset in range(1, ys):
        other = lax.rem(part + offset, ys)
        add_block(other, other * feat, first, slot, second, slot + 1)
        for side in range(2):
            acc_copies.append(
                pltpu.make_async_remote_copy(
                    src_ref=acc.at[other, pl.ds(side * half, half)],
                    dst_ref=acc_in.at[offset - 1, pl.ds(side * half, half)],
                    send_sem=acc_send.at[offset - 1, side],
                    recv_sem=acc_recv.at[offset - 1, side],
                    device_id=device_at(tile, other),
                    device_id_type=MESH,
                )
            )
            acc_copies[-1].start()
    add_block(part, part * feat, first, slot, second, slot + 1)

    def feat_copy(offset, side, sender):
        return pltpu.make_async_remote_copy(
            src_ref=feats.at[sender, pl.ds(side * half, half)],
            dst_ref=feats.at[sender, pl.ds(side * half, half)],
            send_sem=feat_send.at[offset - 1, side],
            recv_sem=feat_recv.at[offset - 1, side],
            device_id=device_at(tile, lax.rem(part + offset, ys)),
            device_id_type=MESH,
        )

    for side in range(2):
        span = slice(side * half, (side + 1) * half)
        total = acc[part, span, :]
        for offset in range(1, ys):
            acc_copies[2 * (offset - 1) + side].wait_recv()
            total = total + acc_in[offset - 1, span, :]
        values = total.astype(jnp.bfloat16).astype(jnp.float32)
        acc[part, span, :] = values
        feats[part, span, :] = (values * gain[...].astype(jnp.float32)[None, :]).astype(jnp.bfloat16)
        for offset in range(1, ys):
            feat_copy(offset, side, part).start()

    def wait_feats(side):
        for offset in range(1, ys):
            feat_copy(offset, side, lax.rem(part + ys - offset, ys)).wait_recv()

    def project(owner, start, size):
        result = jnp.dot(
            feats[0, pl.ds(start, size), :],
            qkv_buf[owner, :feat, :],
            preferred_element_type=jnp.float32,
        )
        for block in range(1, ys):
            result = result + jnp.dot(
                feats[block, pl.ds(start, size), :],
                qkv_buf[owner, block * feat : (block + 1) * feat, :],
                preferred_element_type=jnp.float32,
            )
        return result

    def message_copy(direction, index):
        return pltpu.make_async_remote_copy(
            src_ref=out_msg.at[direction, index],
            dst_ref=in_msg.at[direction, index],
            send_sem=msg_send.at[direction, index],
            recv_sem=msg_recv.at[direction, index],
            device_id=ahead[direction],
            device_id_type=MESH,
        )

    def message(index, with_arrived, first=False):
        distance = half_ring - (index + 1) // 2
        for direction in range(2):
            if first:
                wait_feats(direction)
            odd = lax.rem(index, 2)
            token_half = odd if direction == 0 else 1 - odd
            owner = tile_at(1 - direction, distance)
            value = project(owner, pl.multiple_of(token_half * half, half), half)
            if with_arrived:
                message_copy(direction, index - 2).wait_recv()
                value = value + in_msg[direction, index - 2].astype(jnp.float32)
            out_msg[direction, index] = value.astype(jnp.bfloat16)
            message_copy(direction, index).start()

    messages = 2 * half_ring - 1

    def later_messages(index, carry):
        message(index, True)
        return carry

    for owner in range(xs):
        qkv_copy(owner).wait()
    message(0, False, True)
    message(1, False)

    upright = acc[part].T
    res_buf[...] = upright.astype(jnp.bfloat16)
    stream_copy = pltpu.make_async_copy(res_buf, stream_out, local_sem.at[2])
    stream_copy.start()
    sums[...] = jnp.broadcast_to(jnp.sum(upright * upright, axis=0, keepdims=True), sums.shape)
    sum_copies = []
    for offset in range(1, ys):
        sum_copies.append(
            pltpu.make_async_remote_copy(
                src_ref=sums,
                dst_ref=pair_sums.at[offset - 1],
                send_sem=psum_send.at[offset - 1],
                recv_sem=psum_recv.at[offset - 1],
                device_id=device_at(tile, lax.rem(part + offset, ys)),
                device_id_type=MESH,
            )
        )
        sum_copies[-1].start()
    lax.fori_loop(2, messages - 3, later_messages, 0)

    for copy in sum_copies:
        copy.wait_recv()
    tile_sums = sums[...]
    for offset in range(1, ys):
        tile_sums = tile_sums + pair_sums[offset - 1]
    ring_sums[0] = tile_sums
    for offset in range(1, xs):
        sum_copies.append(
            pltpu.make_async_remote_copy(
                src_ref=ring_sums.at[0],
                dst_ref=ring_sums.at[offset],
                send_sem=rsum_send.at[offset - 1],
                recv_sem=rsum_recv.at[offset - 1],
                device_id=device_at(lax.rem(tile + offset, xs), part),
                device_id_type=MESH,
            )
        )
        sum_copies[-1].start()

    lax.fori_loop(messages - 3, messages, later_messages, 0)

    own[...] = project(tile, 0, tokens)
    for copy in sum_copies[ys - 1 :]:
        copy.wait_recv()
    all_sums = ring_sums[0]
    for offset in range(1, xs):
        all_sums = all_sums + ring_sums[offset]
    inv_rms = lax.rsqrt(all_sums[0:1] / (feat * xs * ys) + 1e-05)
    for index in range(messages - 2, messages):
        for direction in range(2):
            token_half = index % 2 if direction == 0 else 1 - index % 2
            message_copy(direction, index).wait_recv()
            own[token_half * half : (token_half + 1) * half, :] += in_msg[
                direction, index
            ].astype(jnp.float32)
    qkv_out[...] = (own[...].T * inv_rms).astype(jnp.bfloat16)

    for direction in range(2):
        for item in range(arrivals):
            gather_copy(direction, item, tile, 0, window(tile, 0)).wait_send()
        for index in range(messages):
            message_copy(direction, index).wait_send()
    for copy in acc_copies + sum_copies:
        copy.wait_send()
    stream_copy.wait()
    for offset in range(1, ys):
        for side in range(2):
            feat_copy(offset, side, part).wait_send()


def hand_over_kernel(stream, qkv, stream_out, qkv_out, sem):
    moves = [
        pltpu.make_async_copy(source, target, sem.at[lane])
        for lane, (source, target) in enumerate(((stream, stream_out), (qkv, qkv_out)))
    ]
    for move in moves:
        move.start()
    for move in moves:
        move.wait()


def hand_over(stream, qkv):
    return pl.pallas_call(
        hand_over_kernel,
        out_shape=tuple(jax.ShapeDtypeStruct(a.shape, a.dtype) for a in (stream, qkv)),
        in_specs=[pl.BlockSpec(memory_space=pltpu.VMEM)] * 2,
        out_specs=(pl.BlockSpec(memory_space=pl.ANY),) * 2,
        scratch_shapes=[pltpu.SemaphoreType.DMA((2,))],
    )(stream, qkv)


def fused(hidden, residual, w_down, gain, w_qkv):
    gx = lax.axis_size("gx")
    xs, ys = XS, gx // XS
    rows, tokens = hidden.shape
    feat = residual.shape[0]
    cols = w_qkv.shape[2] // xs
    cuts = next(c for c in (6, 4, 2) if rows % (16 * c) == 0)
    width = next(w for w in (512, 256, 128) if feat % w == 0)
    arrivals = cuts * (xs // 2 - 1) + cuts // 2
    messages = xs - 1
    others = max(ys - 1, 1)
    dma = pltpu.SemaphoreType.DMA
    flops = 2 * tokens * (w_down.shape[1] * w_down.shape[2] + w_qkv.shape[1] * w_qkv.shape[2])
    results = pl.pallas_call(
        functools.partial(fused_kernel, xs, ys, cuts, width),
        out_shape=(
            jax.ShapeDtypeStruct((feat, tokens), jnp.bfloat16),
            jax.ShapeDtypeStruct((cols, tokens), jnp.bfloat16),
        ),
        in_specs=[
            pl.BlockSpec(memory_space=pl.ANY),
            pl.BlockSpec(memory_space=pl.ANY),
            pl.BlockSpec(memory_space=pl.ANY),
            pl.BlockSpec(memory_space=pltpu.VMEM),
            pl.BlockSpec(memory_space=pl.ANY),
        ],
        out_specs=(
            pl.BlockSpec(memory_space=pl.ANY),
            pl.BlockSpec(memory_space=pltpu.VMEM),
        ),
        scratch_shapes=[
            pltpu.VMEM((xs, rows, tokens), jnp.bfloat16),
            pltpu.VMEM((feat, tokens), jnp.bfloat16),
            pltpu.VMEM((4, rows // cuts, ys * feat), jnp.bfloat16),
            pltpu.VMEM((xs, ys * feat, cols), jnp.bfloat16),
            pltpu.VMEM((ys, tokens, feat), jnp.float32),
            pltpu.VMEM((others, tokens, feat), jnp.float32),
            pltpu.VMEM((ys, tokens, feat), jnp.bfloat16),
            pltpu.VMEM((8, tokens), jnp.float32),
            pltpu.VMEM((others, 8, tokens), jnp.float32),
            pltpu.VMEM((xs, 8, tokens), jnp.float32),
            pltpu.VMEM((2, messages, tokens // 2, cols), jnp.bfloat16),
            pltpu.VMEM((2, messages, tokens // 2, cols), jnp.bfloat16),
            pltpu.VMEM((tokens, cols), jnp.float32),
            dma((3,)),
            dma((4,)),
            dma((xs,)),
            dma((2, arrivals)),
            dma((2, arrivals)),
            dma((others, 2)),
            dma((others, 2)),
            dma((others, 2)),
            dma((others, 2)),
            dma((others,)),
            dma((others,)),
            dma((xs - 1,)),
            dma((xs - 1,)),
            dma((2, messages)),
            dma((2, messages)),
        ],
        compiler_params=pltpu.CompilerParams(
            collective_id=0, has_side_effects=True, vmem_limit_bytes=66 * 10**6
        ),
        cost_estimate=pl.CostEstimate(
            flops=flops,
            bytes_accessed=2 * (w_down.size + w_qkv.size),
            transcendentals=0,
        ),
    )(hidden, residual, w_down[0], gain, w_qkv[0])
    return hand_over(*results)


def on_device(hidden, residual, w_down, gain, w_qkv):
    cols = w_qkv.shape[2] // XS
    aligned = (
        hidden.shape[0] % 32 == 0
        and hidden.shape[1] % 32 == 0
        and residual.shape[0] % 128 == 0
        and cols % 128 == 0
    )
    step = fused if aligned else permuted
    return step(hidden, residual, w_down, gain, w_qkv)


def solution(mesh):
    placed = (
        P("gx", "groups"),
        P("gx", "groups"),
        P("gx", None, None),
        P("gx"),
        P("gx", None, None),
    )
    return jax.shard_map(
        on_device,
        mesh=mesh,
        in_specs=placed,
        out_specs=(P("gx", "groups"), P("gx", "groups")),
        check_vma=False,
    )
```

```python
import functools

import jax
import jax.numpy as jnp
from jax import lax
from jax.experimental import pallas as pl
from jax.experimental.pallas import tpu as pltpu
from jax.sharding import PartitionSpec as P

D = 16384
XS = 8
MESH = pl.DeviceIdType.MESH


def swapped(block, axis, stride):
    count = lax.axis_size(axis)
    route = []
    for low in range(count):
        high = low | 1 << stride
        if high != low and high < count:
            route += [(low, high), (high, low)]
    return lax.ppermute(block, axis, route)


def for_sending(value):
    return jax.tree.map(lambda a: a.astype(jnp.bfloat16) if a.dtype == jnp.float32 else a, value)


def bit_of(dev_index, position):
    return dev_index // 2**position % 2


def collect_bits(current, positions, dev_index, send_fn):
    for position in positions:
        received = send_fn(current, position)
        high_bit = bit_of(dev_index, position) == 1
        current = jax.tree.map(
            lambda own_part, their_part: jnp.where(
                high_bit,
                jnp.concatenate([their_part, own_part], 0),
                jnp.concatenate([own_part, their_part], 0),
            ),
            current,
            received,
        )
    return current


def halve_bits(partial_value, first_bit, bit_count, bit_order, dev_index, send_fn):
    trailing = partial_value.shape[1:]
    shaped = partial_value.reshape(
        (2,) * bit_count + (partial_value.shape[0] // 2**bit_count,) + trailing
    )
    remaining = list(range(bit_count - 1, -1, -1))
    for relative in bit_order:
        axis_pos = sum([1 for other in remaining if other > relative])
        high_bit = bit_of(dev_index, first_bit + relative)
        retained = lax.dynamic_index_in_dim(shaped, high_bit, axis_pos, keepdims=False)
        outgoing = lax.dynamic_index_in_dim(shaped, 1 - high_bit, axis_pos, keepdims=False)
        shaped = retained + send_fn(outgoing, first_bit + relative)
        remaining = [other for other in remaining if other != relative]
    return shaped


def permuted(hidden, residual, w_down, gain, w_qkv):
    dev_index = lax.axis_index("gx")
    y_bits = (lax.axis_size("gx") // XS).bit_length() - 1
    x_bits = XS.bit_length() - 1
    x_positions = list(range(y_bits, y_bits + x_bits))
    y_positions = list(range(y_bits))
    tile_down = w_down[0]
    tile_qkv = w_qkv[0]
    gathered = collect_bits(
        hidden, x_positions, dev_index, lambda current, position: swapped(current, "gx", position)
    )
    partial_down = lax.dot_general(
        tile_down, gathered, (((0,), (0,)), ((), ())), preferred_element_type=jnp.float32
    )
    down_order = list(range(y_bits - 1, -1, -1))
    down = halve_bits(
        partial_down,
        0,
        y_bits,
        down_order,
        dev_index,
        lambda current, position: swapped(current, "gx", position),
    )
    stream = (residual.astype(jnp.float32) + down).astype(jnp.bfloat16)
    block_stream, block_gain = collect_bits(
        (stream, gain),
        y_positions,
        dev_index,
        lambda current, position: jax.tree.map(
            lambda part, own: part.astype(own.dtype),
            swapped(for_sending(current), "gx", position),
            current,
        ),
    )
    block_values = block_stream.astype(jnp.float32)
    sumsq = jnp.sum(block_values * block_values, axis=0)
    for position in x_positions:
        sumsq = sumsq + swapped(sumsq, "gx", position)
    inv_rms = lax.rsqrt(sumsq / D + 1e-05)
    block_normed = (
        block_values * block_gain.astype(jnp.float32)[:, None] * inv_rms[None, :]
    ).astype(jnp.bfloat16)
    partial_qkv = lax.dot_general(
        tile_qkv, block_normed, (((0,), (0,)), ((), ())), preferred_element_type=jnp.float32
    )
    qkv_order = list(range(x_bits - 1, -1, -1))
    qkv = halve_bits(
        partial_qkv,
        y_bits,
        x_bits,
        qkv_order,
        dev_index,
        lambda current, position: swapped(current, "gx", position),
    )
    return (stream, qkv.astype(jnp.bfloat16))


def ring_position(tile, count):
    odd = lax.rem(tile, 2)
    step = tile // 2
    return (1 - odd) * step + odd * (count - 1 - step)


def ring_tile(position, count):
    back = position // (count // 2)
    return (1 - back) * (2 * position) + back * (2 * (count - 1 - position) + 1)


def fused_kernel(
    xs,
    ys,
    cuts,
    width,
    hidden,
    residual,
    w_down,
    gain,
    w_qkv,
    stream_out,
    qkv_out,
    held,
    res_buf,
    down_buf,
    qkv_buf,
    acc,
    acc_in,
    feats,
    sums,
    pair_sums,
    ring_sums,
    out_msg,
    in_msg,
    own,
    local_sem,
    down_sem,
    qkv_sem,
    ring_send,
    ring_recv,
    acc_send,
    acc_recv,
    feat_send,
    feat_recv,
    psum_send,
    psum_recv,
    rsum_send,
    rsum_recv,
    msg_send,
    msg_recv,
):
    me = lax.axis_index("gx")
    tile, part = me // ys, lax.rem(me, ys)
    place = ring_position(tile, xs)
    rows = hidden.shape[0]
    cut = rows // cuts
    tokens = hidden.shape[1]
    feat = residual.shape[0]
    cols = qkv_out.shape[0]
    half_ring = xs // 2
    half = tokens // 2

    def device_at(x, y):
        return {"gx": x * ys + y}

    def tile_at(direction, distance):
        return ring_tile(lax.rem(place + (2 * direction - 1) * distance + xs, xs), xs)

    ahead = [device_at(tile_at(1, 1), part), device_at(tile_at(0, 1), part)]

    def arrival(direction, item):
        piece = tile_at(direction, item // cuts + 1)
        order = lax.rem(item, cuts)
        return piece, order if direction == 0 else cuts - 1 - order

    def window(piece, chunk):
        return held.at[piece, pl.ds(pl.multiple_of(chunk * cut, cut), cut)]

    def gather_copy(direction, item, piece, chunk, source):
        return pltpu.make_async_remote_copy(
            src_ref=source,
            dst_ref=window(piece, chunk),
            send_sem=ring_send.at[direction, item],
            recv_sem=ring_recv.at[direction, item],
            device_id=ahead[direction],
            device_id_type=MESH,
        )

    def down_copy(slot, piece, chunk):
        start = pl.multiple_of(piece * rows + chunk * cut, cut)
        return pltpu.make_async_copy(
            w_down.at[pl.ds(start, cut)], down_buf.at[slot], down_sem.at[slot]
        )

    def qkv_copy(owner):
        return pltpu.make_async_copy(
            w_qkv.at[:, pl.ds(owner * cols, cols)], qkv_buf.at[owner], qkv_sem.at[owner]
        )

    barrier = pltpu.get_barrier_semaphore()
    for offset in range(1, xs):
        pl.semaphore_signal(
            barrier,
            inc=1,
            device_id=device_at(lax.rem(tile + offset, xs), part),
            device_id_type=MESH,
        )
    for offset in range(1, ys):
        pl.semaphore_signal(
            barrier,
            inc=1,
            device_id=device_at(tile, lax.rem(part + offset, ys)),
            device_id_type=MESH,
        )
    pl.semaphore_wait(barrier, xs - 1 + ys - 1)

    arrivals = cuts * (half_ring - 1) + cuts // 2


    def send_own(direction, item):
        chunk = item if direction == 0 else cuts - 1 - item
        start = pl.multiple_of(chunk * cut, cut)
        gather_copy(direction, item, tile, chunk, hidden.at[pl.ds(start, cut)]).start()

    ahead_by = min(3, cuts)
    for item in range(ahead_by):
        for direction in range(2):
            send_own(direction, item)
    own_copy = pltpu.make_async_copy(hidden, held.at[tile], local_sem.at[0])
    own_copy.start()
    res_copy = pltpu.make_async_copy(residual, res_buf, local_sem.at[1])
    res_copy.start()
    for lane in range(2):
        down_copy(lane, tile, lane).start()
    acc[...] = jnp.zeros_like(acc)
    res_copy.wait()
    acc[part] = res_buf[...].astype(jnp.float32).T
    own_copy.wait()

    def transposed(piece, chunk):
        return held[piece, pl.ds(pl.multiple_of(chunk * cut, cut), cut), :].T

    def add_block(block, base, first, first_slot, second, second_slot):
        for start in range(0, feat, width):
            at = pl.ds(pl.multiple_of(base + start, width), width)
            acc[block, :, start : start + width] += jnp.dot(
                first, down_buf[first_slot, :, at], preferred_element_type=jnp.float32
            ) + jnp.dot(second, down_buf[second_slot, :, at], preferred_element_type=jnp.float32)

    def own_pair(pair, carry):
        slot = lax.rem(pair, 2) * 2
        following = 2 - slot

        @pl.when(pair + 1 < cuts // 2)
        def _():
            for lane in range(2):
                down_copy(following + lane, tile, 2 * pair + 2 + lane).start()

        @pl.when(pair + 1 == cuts // 2)
        def _():
            for lane in range(2):
                down_copy(following + lane, *arrival(lane, 0)).start()

        for lane in range(2):
            down_copy(slot + lane, tile, 2 * pair + lane).wait()
        first, second = transposed(tile, 2 * pair), transposed(tile, 2 * pair + 1)
        for block in range(ys):
            add_block(block, block * feat, first, slot, second, slot + 1)
        return carry

    lax.fori_loop(0, cuts // 2, own_pair, 0)
    for owner in range(xs):
        qkv_copy(owner).start()

    def receive(item, forward):
        for direction in range(2):
            piece, chunk = arrival(direction, item)
            gather_copy(direction, item, piece, chunk, window(piece, chunk)).wait_recv()
            if forward:

                @pl.when(item + ahead_by < cuts)
                def _():
                    send_own(direction, item + ahead_by)

                @pl.when(jnp.logical_and(item + ahead_by >= cuts, item + ahead_by < arrivals))
                def _():
                    piece, chunk = arrival(direction, item + ahead_by - cuts)
                    gather_copy(
                        direction, item + ahead_by, piece, chunk, window(piece, chunk)
                    ).start()

    def weights_of(item, slot):
        for lane in range(2):
            down_copy(slot + lane, *arrival(lane, item)).wait()

    def ring_pair(item, carry):
        slot = lax.rem(item + cuts // 2, 2) * 2
        following = 2 - slot
        for lane in range(2):
            down_copy(following + lane, *arrival(lane, item + 1)).start()
        receive(item, True)
        weights_of(item, slot)
        first, second = transposed(*arrival(0, item)), transposed(*arrival(1, item))
        for block in range(ys):
            add_block(block, block * feat, first, slot, second, slot + 1)
        return carry

    lax.fori_loop(0, arrivals - 1, ring_pair, 0)

    last = arrivals - 1
    slot = (last + cuts // 2) % 2 * 2
    receive(last, False)
    weights_of(last, slot)
    first, second = transposed(*arrival(0, last)), transposed(*arrival(1, last))
    acc_copies = []
    for offset in range(1, ys):
        other = lax.rem(part + offset, ys)
        add_block(other, other * feat, first, slot, second, slot + 1)
        for side in range(2):
            acc_copies.append(
                pltpu.make_async_remote_copy(
                    src_ref=acc.at[other, pl.ds(side * half, half)],
                    dst_ref=acc_in.at[offset - 1, pl.ds(side * half, half)],
                    send_sem=acc_send.at[offset - 1, side],
                    recv_sem=acc_recv.at[offset - 1, side],
                    device_id=device_at(tile, other),
                    device_id_type=MESH,
                )
            )
            acc_copies[-1].start()
    add_block(part, part * feat, first, slot, second, slot + 1)

    def feat_copy(offset, side, sender):
        return pltpu.make_async_remote_copy(
            src_ref=feats.at[sender, pl.ds(side * half, half)],
            dst_ref=feats.at[sender, pl.ds(side * half, half)],
            send_sem=feat_send.at[offset - 1, side],
            recv_sem=feat_recv.at[offset - 1, side],
            device_id=device_at(tile, lax.rem(part + offset, ys)),
            device_id_type=MESH,
        )

    for side in range(2):
        span = slice(side * half, (side + 1) * half)
        total = acc[part, span, :]
        for offset in range(1, ys):
            acc_copies[2 * (offset - 1) + side].wait_recv()
            total = total + acc_in[offset - 1, span, :]
        values = total.astype(jnp.bfloat16).astype(jnp.float32)
        acc[part, span, :] = values
        feats[part, span, :] = (values * gain[...].astype(jnp.float32)[None, :]).astype(jnp.bfloat16)
        for offset in range(1, ys):
            feat_copy(offset, side, part).start()

    def wait_feats(side):
        for offset in range(1, ys):
            feat_copy(offset, side, lax.rem(part + ys - offset, ys)).wait_recv()

    def project(owner, start, size):
        result = jnp.dot(
            feats[0, pl.ds(start, size), :],
            qkv_buf[owner, :feat, :],
            preferred_element_type=jnp.float32,
        )
        for block in range(1, ys):
            result = result + jnp.dot(
                feats[block, pl.ds(start, size), :],
                qkv_buf[owner, block * feat : (block + 1) * feat, :],
                preferred_element_type=jnp.float32,
            )
        return result

    def message_copy(direction, index):
        return pltpu.make_async_remote_copy(
            src_ref=out_msg.at[direction, index],
            dst_ref=in_msg.at[direction, index],
            send_sem=msg_send.at[direction, index],
            recv_sem=msg_recv.at[direction, index],
            device_id=ahead[direction],
            device_id_type=MESH,
        )

    def message(index, with_arrived, first=False):
        distance = half_ring - (index + 1) // 2
        for direction in range(2):
            if first:
                wait_feats(direction)
            odd = lax.rem(index, 2)
            token_half = odd if direction == 0 else 1 - odd
            owner = tile_at(1 - direction, distance)
            value = project(owner, pl.multiple_of(token_half * half, half), half)
            if with_arrived:
                message_copy(direction, index - 2).wait_recv()
                value = value + in_msg[direction, index - 2].astype(jnp.float32)
            out_msg[direction, index] = value.astype(jnp.bfloat16)
            message_copy(direction, index).start()

    messages = 2 * half_ring - 1

    def later_messages(index, carry):
        message(index, True)
        return carry

    for owner in range(xs):
        qkv_copy(owner).wait()
    message(0, False, True)
    message(1, False)

    upright = acc[part].T
    res_buf[...] = upright.astype(jnp.bfloat16)
    stream_copy = pltpu.make_async_copy(res_buf, stream_out, local_sem.at[2])
    stream_copy.start()
    sums[...] = jnp.broadcast_to(jnp.sum(upright * upright, axis=0, keepdims=True), sums.shape)
    sum_copies = []
    for offset in range(1, ys):
        sum_copies.append(
            pltpu.make_async_remote_copy(
                src_ref=sums,
                dst_ref=pair_sums.at[offset - 1],
                send_sem=psum_send.at[offset - 1],
                recv_sem=psum_recv.at[offset - 1],
                device_id=device_at(tile, lax.rem(part + offset, ys)),
                device_id_type=MESH,
            )
        )
        sum_copies[-1].start()
    lax.fori_loop(2, messages - 3, later_messages, 0)

    for copy in sum_copies:
        copy.wait_recv()
    tile_sums = sums[...]
    for offset in range(1, ys):
        tile_sums = tile_sums + pair_sums[offset - 1]
    ring_sums[0] = tile_sums
    for offset in range(1, xs):
        sum_copies.append(
            pltpu.make_async_remote_copy(
                src_ref=ring_sums.at[0],
                dst_ref=ring_sums.at[offset],
                send_sem=rsum_send.at[offset - 1],
                recv_sem=rsum_recv.at[offset - 1],
                device_id=device_at(lax.rem(tile + offset, xs), part),
                device_id_type=MESH,
            )
        )
        sum_copies[-1].start()

    lax.fori_loop(messages - 3, messages, later_messages, 0)

    own[...] = project(tile, 0, tokens)
    for copy in sum_copies[ys - 1 :]:
        copy.wait_recv()
    all_sums = ring_sums[0]
    for offset in range(1, xs):
        all_sums = all_sums + ring_sums[offset]
    inv_rms = lax.rsqrt(all_sums[0:1] / (feat * xs * ys) + 1e-05)
    for index in range(messages - 2, messages):
        for direction in range(2):
            token_half = index % 2 if direction == 0 else 1 - index % 2
            message_copy(direction, index).wait_recv()
            own[token_half * half : (token_half + 1) * half, :] += in_msg[
                direction, index
            ].astype(jnp.float32)
    qkv_out[...] = (own[...].T * inv_rms).astype(jnp.bfloat16)

    for direction in range(2):
        for item in range(arrivals):
            gather_copy(direction, item, tile, 0, window(tile, 0)).wait_send()
        for index in range(messages):
            message_copy(direction, index).wait_send()
    for copy in acc_copies + sum_copies:
        copy.wait_send()
    stream_copy.wait()
    for offset in range(1, ys):
        for side in range(2):
            feat_copy(offset, side, part).wait_send()


def hand_over_kernel(stream, qkv, stream_out, qkv_out, sem):
    moves = [
        pltpu.make_async_copy(source, target, sem.at[lane])
        for lane, (source, target) in enumerate(((stream, stream_out), (qkv, qkv_out)))
    ]
    for move in moves:
        move.start()
    for move in moves:
        move.wait()


def hand_over(stream, qkv):
    return pl.pallas_call(
        hand_over_kernel,
        out_shape=tuple(jax.ShapeDtypeStruct(a.shape, a.dtype) for a in (stream, qkv)),
        in_specs=[pl.BlockSpec(memory_space=pltpu.VMEM)] * 2,
        out_specs=(pl.BlockSpec(memory_space=pl.ANY),) * 2,
        scratch_shapes=[pltpu.SemaphoreType.DMA((2,))],
    )(stream, qkv)


def fused(hidden, residual, w_down, gain, w_qkv):
    gx = lax.axis_size("gx")
    xs, ys = XS, gx // XS
    rows, tokens = hidden.shape
    feat = residual.shape[0]
    cols = w_qkv.shape[2] // xs
    cuts = next(c for c in (6, 4, 2) if rows % (16 * c) == 0)
    width = next(w for w in (512, 256, 128) if feat % w == 0)
    arrivals = cuts * (xs // 2 - 1) + cuts // 2
    messages = xs - 1
    others = max(ys - 1, 1)
    dma = pltpu.SemaphoreType.DMA
    flops = 2 * tokens * (w_down.shape[1] * w_down.shape[2] + w_qkv.shape[1] * w_qkv.shape[2])
    results = pl.pallas_call(
        functools.partial(fused_kernel, xs, ys, cuts, width),
        out_shape=(
            jax.ShapeDtypeStruct((feat, tokens), jnp.bfloat16),
            jax.ShapeDtypeStruct((cols, tokens), jnp.bfloat16),
        ),
        in_specs=[
            pl.BlockSpec(memory_space=pl.ANY),
            pl.BlockSpec(memory_space=pl.ANY),
            pl.BlockSpec(memory_space=pl.ANY),
            pl.BlockSpec(memory_space=pltpu.VMEM),
            pl.BlockSpec(memory_space=pl.ANY),
        ],
        out_specs=(
            pl.BlockSpec(memory_space=pl.ANY),
            pl.BlockSpec(memory_space=pltpu.VMEM),
        ),
        scratch_shapes=[
            pltpu.VMEM((xs, rows, tokens), jnp.bfloat16),
            pltpu.VMEM((feat, tokens), jnp.bfloat16),
            pltpu.VMEM((4, rows // cuts, ys * feat), jnp.bfloat16),
            pltpu.VMEM((xs, ys * feat, cols), jnp.bfloat16),
            pltpu.VMEM((ys, tokens, feat), jnp.float32),
            pltpu.VMEM((others, tokens, feat), jnp.float32),
            pltpu.VMEM((ys, tokens, feat), jnp.bfloat16),
            pltpu.VMEM((8, tokens), jnp.float32),
            pltpu.VMEM((others, 8, tokens), jnp.float32),
            pltpu.VMEM((xs, 8, tokens), jnp.float32),
            pltpu.VMEM((2, messages, tokens // 2, cols), jnp.bfloat16),
            pltpu.VMEM((2, messages, tokens // 2, cols), jnp.bfloat16),
            pltpu.VMEM((tokens, cols), jnp.float32),
            dma((3,)),
            dma((4,)),
            dma((xs,)),
            dma((2, arrivals)),
            dma((2, arrivals)),
            dma((others, 2)),
            dma((others, 2)),
            dma((others, 2)),
            dma((others, 2)),
            dma((others,)),
            dma((others,)),
            dma((xs - 1,)),
            dma((xs - 1,)),
            dma((2, messages)),
            dma((2, messages)),
        ],
        compiler_params=pltpu.CompilerParams(
            collective_id=0, has_side_effects=True, vmem_limit_bytes=66 * 10**6
        ),
        cost_estimate=pl.CostEstimate(
            flops=flops,
            bytes_accessed=2 * (w_down.size + w_qkv.size),
            transcendentals=0,
        ),
    )(hidden, residual, w_down[0], gain, w_qkv[0])
    return hand_over(*results)


def on_device(hidden, residual, w_down, gain, w_qkv):
    cols = w_qkv.shape[2] // XS
    aligned = (
        hidden.shape[0] % 32 == 0
        and hidden.shape[1] % 32 == 0
        and residual.shape[0] % 128 == 0
        and cols % 128 == 0
    )
    step = fused if aligned else permuted
    return step(hidden, residual, w_down, gain, w_qkv)


def solution(mesh):
    placed = (
        P("gx", "groups"),
        P("gx", "groups"),
        P("gx", None, None),
        P("gx"),
        P("gx", None, None),
    )
    return jax.shard_map(
        on_device,
        mesh=mesh,
        in_specs=placed,
        out_specs=(P("gx", "groups"), P("gx", "groups")),
        check_vma=False,
    )
```
